32 devices in a mesh: row: 4 (over y, core), col: 8 (over z, x).
Axes of the slice: x: 2, y: 2, z: 4, core: 2. Of those that a mesh axis runs over, the one named last changes fastest.
Arguments:
- matrix: float32 [4, 4, 8, 256, 256], P(None, 'row', 'col'), as said below
- present: int32 [4, 4, 8], P(None, 'row', 'col'), may hold values from 0 to 1, as said below
- update: int32 [2, 4, 4, 8], P(None, None, 'row', 'col'), may hold values from 0 to 1, as said below
Outputs:
- factored: float32 [4, 4, 8, 256, 256], P(None, 'row', 'col')
The draws below stay inside these ranges and needn't reach their ends.
Inputs may be any that keep to these rules, and one draw needn't show every extreme that they name: `present`: listed tiles lie on or below the diagonal (row >= column). Tiles (0, 0), (1, 0), (1, 1) and every diagonal tile (c, c) of the window, that is with c < 16 and c < 8, are listed; in column 1 every row i >= 1 whose tile in column 0 is listed is listed too. update[k, s, r, c] is 1 exactly where c > k and the tiles (i, c), (i, k) and (c, k) are all listed, with i = r + 4 s. `matrix`: unlisted tiles are zero. Tile (0, 0) is symmetric positive definite, and so is tile (1, 1) minus P0(1) P0(1)^T.
All inputs are finite; a program needn't handle non-finite values.
Results may differ from the reference program's by a relative error of at most 0.0001.
Values sent between devices are 32-bit elements; how exact they have to be, the bound alone decides.
A program may use at most 64 MiB of HBM per device.

```python
import math
import jax
import jax.numpy as jnp
from jax import lax

B = 256
SLOTS = 4
N_ROW = 4
N_COL = 8


def tile_layout(base_key):
    structure_key = jax.random.fold_in(base_key, 101)
    tile_row = jnp.arange(SLOTS)[:, None, None] * N_ROW + jnp.arange(N_ROW)[None, :, None]
    tile_col = jnp.arange(N_COL)[None, None, :]
    coin_flip = jax.random.randint(structure_key, (SLOTS, N_ROW, N_COL), 0, 4)
    first_col = (tile_col == 0) & ((coin_flip < 3) | (tile_row <= 1))
    first_rows = first_col[:, :, 0]
    second = (tile_col == 1) & (tile_row >= 1) & (first_rows[:, :, None] | (coin_flip == 0))
    trailing = (tile_col >= 2) & (tile_row >= tile_col) & ((coin_flip < 2) | (tile_row == tile_col))
    listed = first_col | second | trailing
    updates = []
    for panel in range(2):
        along_col = listed[:, :, panel]
        top_rows = along_col.reshape(SLOTS * N_ROW)[:N_COL]
        if SLOTS * N_ROW < N_COL:
            top_rows = jnp.concatenate([top_rows, jnp.zeros((N_COL - SLOTS * N_ROW,), bool)])
        flag_set = listed & along_col[:, :, None] & top_rows[None, None, :] & (tile_col > panel)
        updates.append(flag_set)
    return (listed.astype(jnp.int32), jnp.stack(updates).astype(jnp.int32))


def draw_present(key, part):
    return tile_layout(key)[0]


def draw_update(key, part):
    return tile_layout(key)[1]


def draw_matrix(key, part):
    listed = tile_layout(key)[0]
    float_key = jax.random.fold_in(key, 202)
    first_key, second_key, third_key = jax.random.split(float_key, 3)
    shape = (SLOTS, N_ROW, N_COL, B, B)
    tile_row = (jnp.arange(SLOTS)[:, None, None] * N_ROW + jnp.arange(N_ROW)[None, :, None])[:, :, :, None, None]
    tile_col = jnp.arange(N_COL)[None, None, :, None, None]
    on_diag = jnp.arange(B)[:, None] == jnp.arange(B)[None, :]
    noise = jax.random.uniform(first_key, shape, jnp.float32, -1.0, 1.0)
    symmetric = 0.5 * (noise + jnp.swapaxes(noise, -1, -2))
    level = jax.random.uniform(second_key, shape, jnp.float32, 0.0, 1.0)
    diagonal_tile = jnp.where(on_diag, 4.0 * (1.0 + 0.5 * level), symmetric * (2.0 / math.sqrt(B)))
    coupling_tile = jnp.where(on_diag, 1.5 * (2.0 * level - 1.0), noise * (0.5 / B))
    general = jnp.clip(jax.random.normal(third_key, shape, jnp.float32), -6.0, 6.0)
    value = jnp.where(tile_row == tile_col, diagonal_tile, jnp.where((tile_row == 1) & (tile_col == 0), coupling_tile, jnp.where(tile_col <= 1, 0.25 * general, general)))
    return value * listed[:, :, :, None, None].astype(jnp.float32)


def setup_inputs(seed: int = 0) -> dict:
    splits = jax.random.split(jax.random.key(seed), 4)
    matrix = draw_matrix(jax.random.fold_in(splits[3], 71), 0)
    present = draw_present(jax.random.fold_in(splits[3], 71), 0)
    update = draw_update(jax.random.fold_in(splits[3], 71), 0)
    return dict(matrix=matrix, present=present, update=update)


def solve_panel(factor, blocks):
    count = blocks.shape[0]
    width = blocks.shape[-1]
    stacked = jnp.transpose(blocks, (2, 0, 1)).reshape(width, count * width)
    solved = jax.scipy.linalg.solve_triangular(factor, stacked, lower=True)
    return jnp.transpose(solved.reshape(width, count, width), (1, 2, 0))

def reference(matrix, present, update):
    slot_count = matrix.shape[0]
    row_count = matrix.shape[1]
    col_count = matrix.shape[2]
    width = matrix.shape[-1]
    tile_data = matrix
    for panel in range(2):
        factor = jnp.linalg.cholesky(tile_data[0, panel, panel])
        column = tile_data[:, :, panel].reshape(slot_count * row_count, width, width)
        solved = solve_panel(factor, column)
        solved = solved.at[panel].set(factor)
        far_tiles = solved[:col_count]
        if far_tiles.shape[0] < col_count:
            filler = jnp.zeros((col_count - far_tiles.shape[0], width, width), jnp.float32)
            far_tiles = jnp.concatenate([far_tiles, filler], 0)
        solved_grid = solved.reshape(slot_count, row_count, width, width)
        tile_data = tile_data.at[:, :, panel].set(solved_grid)
        pair_flags = update[panel].astype(jnp.float32)
        blocks = []
        for slot in range(slot_count):
            product = jnp.einsum('rab,cdb->rcad', solved_grid[slot], far_tiles, precision=lax.Precision.HIGHEST)
            blocks.append(tile_data[slot] - pair_flags[slot][:, :, None, None] * product)
        tile_data = jnp.stack(blocks)
    return tile_data * present.astype(jnp.float32)[:, :, :, None, None]
```

```python
import functools

import jax
import jax.numpy as jnp
from jax import lax
from jax.experimental import pallas as pl
from jax.experimental.pallas import tpu as pltpu
from jax.sharding import PartitionSpec as P

MESH = pl.DeviceIdType.MESH
HI = lax.Precision.HIGHEST
NB = 64
GROUP = 4


def dot(a, b, contract):
    return lax.dot_general(
        a, b, (contract, ((), ())), precision=HI, preferred_element_type=jnp.float32
    )


def nn(a, b):
    return dot(a, b, ((1,), (0,)))


def nt(a, b):
    return dot(a, b, ((1,), (1,)))


def tn(a, b):
    return dot(a, b, ((0,), (0,)))


def invert_block(m):
    n = m.shape[0]
    done = []
    for k in range(0, n, GROUP):
        top = (k // 8) * 8
        off = k - top
        cols = [jnp.broadcast_to(m[:, k + t : k + t + 1], m.shape) for t in range(GROUP)]
        rows = [m[off + t : off + t + 1, :] for t in range(GROUP)]
        total = None
        for t in range(GROUP):
            pivot = cols[t][off + t : off + t + 1, :]
            inverse = 1.0 / pivot
            done.append(rows[t] * lax.rsqrt(pivot))
            scaled = rows[t] * inverse
            for u in range(t + 1, GROUP):
                entry = cols[u][off + t : off + t + 1, :]
                rows[u] = rows[u] - entry * scaled
                cols[u] = cols[u] - cols[t] * (entry * inverse)
            term = cols[t] * scaled
            total = term if total is None else total + term
        m = m - total
        if (k + GROUP) % 8 == 0:
            m = m[8:]
    return jnp.concatenate(done, axis=0)


def inverse_factor(work, block_inv):
    width = work.shape[0]
    blocks = width // NB

    def step(j, carry):
        rows = pl.ds(pl.multiple_of(j * NB, NB), NB)
        strip = work[rows, :]
        diag = strip[:, :NB]
        for b in range(1, blocks):
            diag = jnp.where(j == b, strip[:, b * NB : (b + 1) * NB], diag)
        eye = (
            lax.broadcasted_iota(jnp.int32, (NB, NB), 0)
            == lax.broadcasted_iota(jnp.int32, (NB, NB), 1)
        ).astype(jnp.float32)
        solved = invert_block(jnp.concatenate([diag, eye], axis=1))
        block = solved[:, NB:]
        strip = nn(block, strip)
        lane = lax.broadcasted_iota(jnp.int32, (NB, width), 1)
        upper = jnp.where(lane >= (j + 1) * NB, strip[:, :width], 0.0)
        work[...] = work[...] - tn(upper, strip)
        work[rows, :] = strip
        return carry

    lax.fori_loop(0, blocks, step, 0)


def kernel(
    n_row, n_col, m_ref, listed, update, o_ref, dbuf, far, lead, bc, work, wcol, acc, wfar, p0far,
    d_send, d_recv, far_send, far_recv, lead_send, lead_recv, bc_send, bc_recv,
):
    r = lax.axis_index("row")
    c = lax.axis_index("col")
    slots, width = m_ref.shape[0], m_ref.shape[-1]
    half = width // 2
    x = c % 2
    cross = c + 1 - 2 * x
    root = (r == 0) & (c == 0)
    lead_b = (r == 1) & (c == 1)
    far_row = c % n_row
    far_slot = jnp.minimum(c // n_row, slots - 1)

    def greet(row, col):
        pl.semaphore_signal(
            pltpu.get_barrier_semaphore(), inc=1, device_id=(row, col), device_id_type=MESH
        )

    barrier = pltpu.get_barrier_semaphore()
    for k in range(1, n_row):
        greet((r + k) % n_row, c)
    greet(r, cross)
    partners = n_row + (c >= 2).astype(jnp.int32) + (c + 2 < n_col).astype(jnp.int32)

    @pl.when(c >= 2)
    def _():
        greet(r, c - 2)

    @pl.when(c + 2 < n_col)
    def _():
        greet(r, c + 2)

    @pl.when(root)
    def _():
        greet(1, 1)

    @pl.when(lead_b)
    def _():
        greet(0, 0)

    @pl.when(c < 2)
    def _():
        dbuf[x] = m_ref[...]

    pl.semaphore_wait(barrier, partners + (root | lead_b).astype(jnp.int32))

    def lead_copy(q):
        return pltpu.make_async_remote_copy(
            m_ref.at[0], lead.at[q], lead_send.at[q], lead_recv.at[q],
            device_id=(0, 0), device_id_type=MESH,
        )

    lead_a = (r == 1) & (c == 0)

    @pl.when(lead_a)
    def _():
        lead_copy(0).start()

    @pl.when(lead_b)
    def _():
        lead_copy(1).start()

    def line_copy(s):
        return pltpu.make_async_remote_copy(
            dbuf.at[x, s], dbuf.at[x, s], d_send.at[0, s], d_recv.at[0, s],
            device_id=(r, c + 2), device_id_type=MESH,
        )

    def cross_copy(s, side):
        return pltpu.make_async_remote_copy(
            dbuf.at[side, s], dbuf.at[side, s], d_send.at[1, s], d_recv.at[1, s],
            device_id=(r, cross), device_id_type=MESH,
        )

    def line_need(col, s):
        return (col >= 2) & (col < n_col) & (r + n_row * s >= col - col % 2)

    def cross_need(col, s):
        return (col >= 1) & (r + n_row * s >= col)

    for s in range(slots):

        @pl.when(line_need(c, s))
        def _():
            line_copy(s).wait_recv()

        @pl.when(line_need(c + 2, s))
        def _():
            line_copy(s).start()

        @pl.when(cross_need(cross, s))
        def _():
            cross_copy(s, x).start()

    child = [
        ((r % 2 == 0) & (c == 0) & (r + 2 < n_row), (r + 2, c)),
        ((r % 2 == 0) & (c + 2 < n_col), (r, c + 2)),
        ((r % 2 == 0) & (c == 0), (r, c + 1)),
        ((r % 2 == 0) & (r + 1 < n_row), (r + 1, c)),
    ]

    def bc_copy(q, h, k):
        piece = bc.at[q, pl.ds(h * half, half)]
        return pltpu.make_async_remote_copy(
            piece, piece, bc_send.at[q, h, k], bc_recv.at[q, h],
            device_id=child[k][1], device_id_type=MESH,
        )

    def bc_start(q, h):
        for k in range(4):

            @pl.when(child[k][0])
            def _():
                bc_copy(q, h, k).start()

    def pass_on(q):
        for h in range(2):

            @pl.when(jnp.logical_not(root))
            def _():
                bc_copy(q, h, 0).wait_recv()
                bc_start(q, h)

    @pl.when(root)
    def _():
        eye = (
            lax.broadcasted_iota(jnp.int32, (width, width), 0)
            == lax.broadcasted_iota(jnp.int32, (width, width), 1)
        ).astype(jnp.float32)
        work[:, :width] = m_ref[0]
        work[:, width:] = eye
        inverse_factor(work, None)
        bc[0] = work[:, width:]
        bc_start(0, 0)
        bc_start(0, 1)
        lead_copy(0).wait_recv()
        lead_copy(1).wait_recv()
        p01 = nt(lead[0], work[:, width:])
        bc[1] = p01
        bc_start(1, 0)
        bc_start(1, 1)
        work[:, :width] = lead[1] - nt(p01, p01)
        work[:, width:] = eye
        inverse_factor(work, None)
        bc[2] = work[:, width:]
        bc_start(2, 0)
        bc_start(2, 1)

    for s in range(slots):

        @pl.when(cross_need(c, s))
        def _():
            cross_copy(s, 1 - x).wait_recv()

    def far_copy(k, q):
        return pltpu.make_async_remote_copy(
            dbuf.at[q, far_slot], far.at[q], far_send.at[k, q], far_recv.at[q],
            device_id=((r + k) % n_row, c), device_id_type=MESH,
        )

    @pl.when((c >= 1) & (r == far_row))
    def _():
        for k in range(1, n_row):
            for q in range(2):
                far_copy(k, q).start()
        for q in range(2):
            far[q] = dbuf[q, far_slot]

    @pl.when((c >= 1) & (r != far_row))
    def _():
        for q in range(2):
            far_copy(1, q).wait_recv()

    pass_on(0)
    pass_on(1)

    lower = lax.broadcasted_iota(jnp.int32, (width, width), 0) >= lax.broadcasted_iota(
        jnp.int32, (width, width), 1
    )

    @pl.when(c >= 2)
    def _():
        p0far[...] = nt(far[0], bc[0])
        wfar[...] = far[1] - nt(p0far[...], bc[1])

    for s in range(slots):
        inside = r + n_row * s >= c

        @pl.when(inside & (c == 0))
        def _():
            panel = nt(m_ref[s], bc[0])
            panel = jnp.where(lower | (r + n_row * s > 0), panel, 0.0)
            o_ref[s] = jnp.where(listed[s] > 0, panel, 0.0)

        @pl.when(inside & (c >= 1))
        def _():
            panel = nt(dbuf[0, s], bc[0])
            wcol[s] = dbuf[1, s] - nt(panel, bc[1])

            @pl.when(c >= 2)
            def _():
                product = nt(panel, p0far[...])
                acc[s] = m_ref[s] - jnp.where(update[s] > 0, product, 0.0)

    pass_on(2)

    @pl.when(c >= 2)
    def _():
        p1far = nt(wfar[...], bc[2])
        p0far[...] = nn(p1far, bc[2])

    for s in range(slots):
        inside = r + n_row * s >= c

        @pl.when(inside & (c == 1))
        def _():
            panel = nt(wcol[s], bc[2])
            panel = jnp.where(lower | (r + n_row * s > 1), panel, 0.0)
            o_ref[s] = jnp.where(listed[s] > 0, panel, 0.0)

        @pl.when(inside & (c >= 2))
        def _():
            product = nt(wcol[s], p0far[...])
            out = acc[s] - jnp.where(update[slots + s] > 0, product, 0.0)
            o_ref[s] = jnp.where(listed[s] > 0, out, 0.0)

        @pl.when(jnp.logical_not(inside))
        def _():
            o_ref[s] = jnp.zeros((width, width), jnp.float32)

    @pl.when(lead_a)
    def _():
        lead_copy(0).wait_send()

    @pl.when(lead_b)
    def _():
        lead_copy(1).wait_send()

    for s in range(slots):

        @pl.when(line_need(c + 2, s))
        def _():
            line_copy(s).wait_send()

        @pl.when(cross_need(cross, s))
        def _():
            cross_copy(s, x).wait_send()

    @pl.when((c >= 1) & (r == far_row))
    def _():
        for k in range(1, n_row):
            for q in range(2):
                far_copy(k, q).wait_send()

    for q in range(3):
        for h in range(2):
            for k in range(4):

                @pl.when(child[k][0])
                def _():
                    bc_copy(q, h, k).wait_send()


def on_device(n_row, n_col, matrix, present, update):
    tiles = matrix[:, 0, 0]
    slots, width = tiles.shape[0], tiles.shape[-1]
    tile = (width, width)
    dma = pltpu.SemaphoreType.DMA
    vmem = pl.BlockSpec(memory_space=pltpu.VMEM)
    smem = pl.BlockSpec(memory_space=pltpu.SMEM)
    out = pl.pallas_call(
        functools.partial(kernel, n_row, n_col),
        out_shape=jax.ShapeDtypeStruct(tiles.shape, jnp.float32),
        in_specs=[vmem, smem, smem],
        out_specs=vmem,
        scratch_shapes=[
            pltpu.VMEM((2, slots) + tile, jnp.float32),
            pltpu.VMEM((2,) + tile, jnp.float32),
            pltpu.VMEM((2,) + tile, jnp.float32),
            pltpu.VMEM((3,) + tile, jnp.float32),
            pltpu.VMEM((width, 2 * width), jnp.float32),
            pltpu.VMEM((slots,) + tile, jnp.float32),
            pltpu.VMEM((slots,) + tile, jnp.float32),
            pltpu.VMEM(tile, jnp.float32),
            pltpu.VMEM(tile, jnp.float32),
            dma((2, slots)),
            dma((2, slots)),
            dma((n_row, 2)),
            dma((2,)),
            dma((2,)),
            dma((2,)),
            dma((3, 2, 4)),
            dma((3, 2)),
        ],
        compiler_params=pltpu.CompilerParams(
            collective_id=0, has_side_effects=True, vmem_limit_bytes=40 * 1024 * 1024
        ),
    )(tiles, present.reshape(slots), update.reshape(2 * slots))
    return out[:, None, None]


def solution(mesh):
    return jax.shard_map(
        functools.partial(on_device, mesh.shape["row"], mesh.shape["col"]),
        mesh=mesh,
        in_specs=(
            P(None, "row", "col", None, None),
            P(None, "row", "col"),
            P(None, None, "row", "col"),
        ),
        out_specs=P(None, "row", "col", None, None),
        check_vma=False,
    )
```

```python
import functools

import jax
import jax.numpy as jnp
from jax import lax
from jax.experimental import pallas as pl
from jax.experimental.pallas import tpu as pltpu
from jax.sharding import PartitionSpec as P

MESH = pl.DeviceIdType.MESH
HI = lax.Precision.HIGHEST
NB = 128
GROUP = 8
PIECES = 4


def dot(a, b, contract):
    return lax.dot_general(
        a, b, (contract, ((), ())), precision=HI, preferred_element_type=jnp.float32
    )


def nn(a, b):
    return dot(a, b, ((1,), (0,)))


def nt(a, b):
    return dot(a, b, ((1,), (1,)))


def tn(a, b):
    return dot(a, b, ((0,), (0,)))


def invert_block(m):
    n = m.shape[0]
    done = []
    for k in range(0, n, GROUP):
        cols = [jnp.broadcast_to(m[:, k + t : k + t + 1], m.shape) for t in range(GROUP)]
        rows = [m[t : t + 1, :] for t in range(GROUP)]
        total = None
        for t in range(GROUP):
            pivot = cols[t][t : t + 1, :]
            inverse = 1.0 / pivot
            done.append(rows[t] * lax.rsqrt(pivot))
            scaled = rows[t] * inverse
            for u in range(t + 1, GROUP):
                entry = cols[u][t : t + 1, :]
                rows[u] = rows[u] - entry * scaled
                cols[u] = cols[u] - cols[t] * (entry * inverse)
            term = cols[t] * scaled
            total = term if total is None else total + term
        m = m - total
        m = m[GROUP:]
    return jnp.concatenate(done, axis=0)


def inverse_factor(a, ready=None):
    n = a.shape[0]
    if n <= NB:
        eye = (
            lax.broadcasted_iota(jnp.int32, (n, n), 0)
            == lax.broadcasted_iota(jnp.int32, (n, n), 1)
        ).astype(jnp.float32)
        return invert_block(jnp.concatenate([a, eye], axis=1))[:, n:]
    h = n // 2
    first = inverse_factor(a[:h, :h])
    if ready is not None:
        ready(first)
    upper = nn(first, a[:h, h:])
    rest = a[h:, h:] - tn(upper, upper)
    below = tn(upper, first)
    last = inverse_factor(rest)
    return jnp.concatenate(
        [
            jnp.concatenate([first, jnp.zeros((h, h), jnp.float32)], axis=1),
            jnp.concatenate([-nn(last, below), last], axis=1),
        ],
        axis=0,
    )


def kernel(
    n_row, n_col, m_ref, listed, update, o_ref, dbuf, far, lead, bc, wcol, acc, wfar, p0far, p01,
    d_send, d_recv, far_send, far_recv, lead_send, lead_recv, bc_send, bc_recv,
):
    r = lax.axis_index("row")
    c = lax.axis_index("col")
    slots, width = m_ref.shape[0], m_ref.shape[-1]
    x = c % 2
    cross = c + 1 - 2 * x
    root = (r == 0) & (c == 0)
    lead_b = (r == 1) & (c == 1)
    far_row = c % n_row
    far_slot = jnp.minimum(c // n_row, slots - 1)

    def greet(row, col):
        pl.semaphore_signal(
            pltpu.get_barrier_semaphore(), inc=1, device_id=(row, col), device_id_type=MESH
        )

    barrier = pltpu.get_barrier_semaphore()
    for k in range(1, n_row):
        greet((r + k) % n_row, c)
    greet(r, cross)
    partners = n_row + (c >= 2).astype(jnp.int32) + (c + 2 < n_col).astype(jnp.int32)

    @pl.when(c >= 2)
    def _():
        greet(r, c - 2)

    @pl.when(c + 2 < n_col)
    def _():
        greet(r, c + 2)

    @pl.when(root)
    def _():
        greet(1, 1)

    @pl.when(lead_b)
    def _():
        greet(0, 0)

    @pl.when(c < 2)
    def _():
        dbuf[x] = m_ref[...]

    pl.semaphore_wait(barrier, partners + (root | lead_b).astype(jnp.int32))

    def lead_copy(q):
        return pltpu.make_async_remote_copy(
            m_ref.at[0], lead.at[q], lead_send.at[q], lead_recv.at[q],
            device_id=(0, 0), device_id_type=MESH,
        )

    lead_a = (r == 1) & (c == 0)

    @pl.when(lead_b)
    def _():
        lead_copy(1).start()

    part = width // PIECES

    def line_copy(s, h):
        piece = dbuf.at[x, s, pl.ds(h * part, part)]
        return pltpu.make_async_remote_copy(
            piece, piece, d_send.at[0, s, h], d_recv.at[0, s, h],
            device_id=(r, c + 2), device_id_type=MESH,
        )

    def cross_copy(s, h, side):
        piece = dbuf.at[side, s, pl.ds(h * part, part)]
        return pltpu.make_async_remote_copy(
            piece, piece, d_send.at[1, s, h], d_recv.at[1, s, h],
            device_id=(r, cross), device_id_type=MESH,
        )

    def line_need(col, s):
        return (col >= 2) & (col < n_col) & (r + n_row * s >= col - col % 2)

    def cross_need(col, s):
        return (col >= 1) & (r + n_row * s >= col)

    def travel(s):
        for h in range(PIECES):

            @pl.when(line_need(c, s))
            def _():
                line_copy(s, h).wait_recv()

            @pl.when(line_need(c + 2, s))
            def _():
                line_copy(s, h).start()

            @pl.when(cross_need(cross, s))
            def _():
                cross_copy(s, h, x).start()

    def arrive(s):
        @pl.when(cross_need(c, s))
        def _():
            for h in range(PIECES):
                cross_copy(s, h, 1 - x).wait_recv()

        @pl.when((c >= 1) & (r == far_row) & (far_slot == s))
        def _():
            for q in range(2):
                for k in range(n_row // 2):
                    far_copy(k, q, dbuf.at[q, s]).start()
                far[q] = dbuf[q, s]

    def far_copy(k, q, source):
        target = r + 1 - 2 * (r % 2) if k == 0 else (r + 2 * k) % n_row
        return pltpu.make_async_remote_copy(
            source, far.at[q], far_send.at[k, q], far_recv.at[q],
            device_id=(target, c), device_id_type=MESH,
        )

    half = width // 2
    quarter = width // 4
    triangle = [(0, half, half, 0), (half, quarter, width, 1), (half + quarter, quarter, width, 0)]
    full = [(h * quarter, quarter, width, h % 2) for h in range(4)]
    pieces = [triangle, full, triangle]
    start_row = [0, 1, 0]

    def child(q, line):
        p = start_row[q]
        mine = r % 2 == p
        over = c % 2 == line
        if line == 1:
            over = (over & jnp.logical_not((r == p) & (c == 1))) | ((r == p) & (c == 0))
        return [
            (mine & over, (r, cross)),
            (mine & (c % 2 == line) & (c + 2 < n_col), (r, c + 2)),
            (mine & (c == line) & (r + 2 < n_row), (r + 2, c)),
            (mine, (r + 1 - 2 * p, c)),
        ]

    def bc_copy(q, h, k):
        row, rows, cols, line = pieces[q][h]
        piece = bc.at[q, pl.ds(row, rows), pl.ds(0, cols)]
        return pltpu.make_async_remote_copy(
            piece, piece, bc_send.at[q, h, k], bc_recv.at[q, h],
            device_id=child(q, line)[k][1], device_id_type=MESH,
        )

    def bc_start(q, h):
        for k in range(4):

            @pl.when(child(q, pieces[q][h][3])[k][0])
            def _():
                bc_copy(q, h, k).start()

    def pass_on(q):
        @pl.when(jnp.logical_not((r == start_row[q]) & (c == 0)))
        def _():
            for h in range(len(pieces[q])):
                bc_copy(q, h, 0).wait_recv()
                bc_start(q, h)

    order = list(range(1, slots)) + [0]

    @pl.when(lead_a)
    def _():
        bc[1] = m_ref[0]
        for h in range(4):
            bc_start(1, h)

    @pl.when(jnp.logical_not(root))
    def _():
        for q in (0, 2):
            bc[q, :half, half:] = jnp.zeros((half, width - half), jnp.float32)

    travel(order[0])

    @pl.when(root)
    def _():
        for s in order[1:]:
            travel(s)

        def ready(q, first):
            bc[q, :half, :half] = first
            bc_start(q, 0)

        def rest(q, inverse):
            bc[q, :half, half:] = jnp.zeros((half, width - half), jnp.float32)
            bc[q, half:, :] = inverse[half:]
            bc_start(q, 1)
            bc_start(q, 2)

        first = inverse_factor(m_ref[0], functools.partial(ready, 0))
        rest(0, first)
        pass_on(1)
        lead_copy(1).wait_recv()
        cross01 = nt(bc[1], first)
        rest(2, inverse_factor(lead[1] - nt(cross01, cross01), functools.partial(ready, 2)))

    @pl.when(jnp.logical_not(root))
    def _():
        pass_on(1)
        arrive(order[0])
        for n, s in enumerate(order[1:]):
            travel(s)
            if n == len(order) - 2:
                pass_on(0)
            arrive(s)

    @pl.when((c >= 1) & (r != far_row))
    def _():
        for q in range(2):
            far_copy(0, q, far.at[q]).wait_recv()

            @pl.when(r % 2 == far_row % 2)
            def _():
                far_copy(0, q, far.at[q]).start()

    p01[...] = nt(bc[1], bc[0])

    lower = lax.broadcasted_iota(jnp.int32, (width, width), 0) >= lax.broadcasted_iota(
        jnp.int32, (width, width), 1
    )

    @pl.when(c >= 2)
    def _():
        p0far[...] = nt(far[0], bc[0])
        wfar[...] = far[1] - nt(p0far[...], p01[...])

    for s in range(slots):
        inside = r + n_row * s >= c

        @pl.when(inside & (c == 0))
        def _():
            panel = nt(m_ref[s], bc[0])
            panel = jnp.where(lower | (r + n_row * s > 0), panel, 0.0)
            o_ref[s] = jnp.where(listed[s] > 0, panel, 0.0)

        @pl.when(inside & (c >= 1))
        def _():
            panel = nt(dbuf[0, s], bc[0])
            wcol[s] = dbuf[1, s] - nt(panel, p01[...])

            @pl.when(c >= 2)
            def _():
                product = nt(panel, p0far[...])
                acc[s] = m_ref[s] - jnp.where(update[s] > 0, product, 0.0)

    @pl.when(jnp.logical_not(root))
    def _():
        pass_on(2)

    @pl.when(c >= 2)
    def _():
        p1far = nt(wfar[...], bc[2])
        p0far[...] = nn(p1far, bc[2])

    for s in range(slots):
        inside = r + n_row * s >= c

        @pl.when(inside & (c == 1))
        def _():
            panel = nt(wcol[s], bc[2])
            panel = jnp.where(lower | (r + n_row * s > 1), panel, 0.0)
            o_ref[s] = jnp.where(listed[s] > 0, panel, 0.0)

        @pl.when(inside & (c >= 2))
        def _():
            product = nt(wcol[s], p0far[...])
            out = acc[s] - jnp.where(update[slots + s] > 0, product, 0.0)
            o_ref[s] = jnp.where(listed[s] > 0, out, 0.0)

        @pl.when(jnp.logical_not(inside))
        def _():
            o_ref[s] = jnp.zeros((width, width), jnp.float32)

    @pl.when(lead_b)
    def _():
        lead_copy(1).wait_send()

    for s in range(slots):
        for h in range(PIECES):

            @pl.when(line_need(c + 2, s))
            def _():
                line_copy(s, h).wait_send()

            @pl.when(cross_need(cross, s))
            def _():
                cross_copy(s, h, x).wait_send()

    @pl.when((c >= 1) & (r == far_row))
    def _():
        for k in range(n_row // 2):
            for q in range(2):
                far_copy(k, q, dbuf.at[q, far_slot]).wait_send()

    @pl.when((c >= 1) & (r != far_row) & (r % 2 == far_row % 2))
    def _():
        for q in range(2):
            far_copy(0, q, far.at[q]).wait_send()

    for q in range(3):
        for h in range(len(pieces[q])):
            for k in range(4):

                @pl.when(child(q, pieces[q][h][3])[k][0])
                def _():
                    bc_copy(q, h, k).wait_send()


def on_device(n_row, n_col, matrix, present, update):
    tiles = matrix[:, 0, 0]
    slots, width = tiles.shape[0], tiles.shape[-1]
    tile = (width, width)
    dma = pltpu.SemaphoreType.DMA
    vmem = pl.BlockSpec(memory_space=pltpu.VMEM)
    smem = pl.BlockSpec(memory_space=pltpu.SMEM)
    out = pl.pallas_call(
        functools.partial(kernel, n_row, n_col),
        out_shape=jax.ShapeDtypeStruct(tiles.shape, jnp.float32),
        in_specs=[vmem, smem, smem],
        out_specs=vmem,
        scratch_shapes=[
            pltpu.VMEM((2, slots) + tile, jnp.float32),
            pltpu.VMEM((2,) + tile, jnp.float32),
            pltpu.VMEM((2,) + tile, jnp.float32),
            pltpu.VMEM((3,) + tile, jnp.float32),
            pltpu.VMEM((slots,) + tile, jnp.float32),
            pltpu.VMEM((slots,) + tile, jnp.float32),
            pltpu.VMEM(tile, jnp.float32),
            pltpu.VMEM(tile, jnp.float32),
            pltpu.VMEM(tile, jnp.float32),
            dma((2, slots, PIECES)),
            dma((2, slots, PIECES)),
            dma((n_row, 2)),
            dma((2,)),
            dma((2,)),
            dma((2,)),
            dma((3, 4, 4)),
            dma((3, 4)),
        ],
        compiler_params=pltpu.CompilerParams(
            collective_id=0, has_side_effects=True, vmem_limit_bytes=40 * 1024 * 1024
        ),
    )(tiles, present.reshape(slots), update.reshape(2 * slots))
    return out[:, None, None]


def solution(mesh):
    return jax.shard_map(
        functools.partial(on_device, mesh.shape["row"], mesh.shape["col"]),
        mesh=mesh,
        in_specs=(
            P(None, "row", "col", None, None),
            P(None, "row", "col"),
            P(None, None, "row", "col"),
        ),
        out_specs=P(None, "row", "col", None, None),
        check_vma=False,
    )
```

```python
import functools

import jax
import jax.numpy as jnp
from jax import lax
from jax.experimental import pallas as pl
from jax.experimental.pallas import tpu as pltpu
from jax.sharding import PartitionSpec as P

MESH = pl.DeviceIdType.MESH
HI = lax.Precision.HIGHEST
NB = 128
GROUP = 8


def dot(a, b, contract):
    return lax.dot_general(
        a, b, (contract, ((), ())), precision=HI, preferred_element_type=jnp.float32
    )


def nn(a, b):
    return dot(a, b, ((1,), (0,)))


def nt(a, b):
    return dot(a, b, ((1,), (1,)))


def tn(a, b):
    return dot(a, b, ((0,), (0,)))


def invert_block(m):
    n = m.shape[0]
    done = []
    for k in range(0, n, GROUP):
        cols = [jnp.broadcast_to(m[:, k + t : k + t + 1], m.shape) for t in range(GROUP)]
        rows = [m[t : t + 1, :] for t in range(GROUP)]
        total = None
        for t in range(GROUP):
            pivot = cols[t][t : t + 1, :]
            inverse = 1.0 / pivot
            done.append(rows[t] * lax.rsqrt(pivot))
            scaled = rows[t] * inverse
            for u in range(t + 1, GROUP):
                entry = cols[u][t : t + 1, :]
                rows[u] = rows[u] - entry * scaled
                cols[u] = cols[u] - cols[t] * (entry * inverse)
            term = cols[t] * scaled
            total = term if total is None else total + term
        m = m - total
        m = m[GROUP:]
    return jnp.concatenate(done, axis=0)


def inverse_factor(a):
    n = a.shape[0]
    if n <= NB:
        eye = (
            lax.broadcasted_iota(jnp.int32, (n, n), 0)
            == lax.broadcasted_iota(jnp.int32, (n, n), 1)
        ).astype(jnp.float32)
        return invert_block(jnp.concatenate([a, eye], axis=1))[:, n:]
    h = n // 2
    first = inverse_factor(a[:h, :h])
    upper = nn(first, a[:h, h:])
    rest = a[h:, h:] - tn(upper, upper)
    below = tn(upper, first)
    last = inverse_factor(rest)
    return jnp.concatenate(
        [
            jnp.concatenate([first, jnp.zeros((h, h), jnp.float32)], axis=1),
            jnp.concatenate([-nn(last, below), last], axis=1),
        ],
        axis=0,
    )


def kernel(
    n_row, n_col, m_ref, listed, update, o_ref, dbuf, far, lead, bc, wcol, acc, wfar, p0far,
    d_send, d_recv, far_send, far_recv, lead_send, lead_recv, bc_send, bc_recv,
):
    r = lax.axis_index("row")
    c = lax.axis_index("col")
    slots, width = m_ref.shape[0], m_ref.shape[-1]
    half = width // 2
    x = c % 2
    cross = c + 1 - 2 * x
    root = (r == 0) & (c == 0)
    lead_b = (r == 1) & (c == 1)
    far_row = c % n_row
    far_slot = jnp.minimum(c // n_row, slots - 1)

    def greet(row, col):
        pl.semaphore_signal(
            pltpu.get_barrier_semaphore(), inc=1, device_id=(row, col), device_id_type=MESH
        )

    barrier = pltpu.get_barrier_semaphore()
    for k in range(1, n_row):
        greet((r + k) % n_row, c)
    greet(r, cross)
    partners = n_row + (c >= 2).astype(jnp.int32) + (c + 2 < n_col).astype(jnp.int32)

    @pl.when(c >= 2)
    def _():
        greet(r, c - 2)

    @pl.when(c + 2 < n_col)
    def _():
        greet(r, c + 2)

    @pl.when(root)
    def _():
        greet(1, 1)

    @pl.when(lead_b)
    def _():
        greet(0, 0)

    @pl.when(c < 2)
    def _():
        dbuf[x] = m_ref[...]

    pl.semaphore_wait(barrier, partners + (root | lead_b).astype(jnp.int32))

    def lead_copy(q):
        return pltpu.make_async_remote_copy(
            m_ref.at[0], lead.at[q], lead_send.at[q], lead_recv.at[q],
            device_id=(0, 0), device_id_type=MESH,
        )

    lead_a = (r == 1) & (c == 0)

    @pl.when(lead_a)
    def _():
        lead_copy(0).start()

    @pl.when(lead_b)
    def _():
        lead_copy(1).start()

    def line_copy(s):
        return pltpu.make_async_remote_copy(
            dbuf.at[x, s], dbuf.at[x, s], d_send.at[0, s], d_recv.at[0, s],
            device_id=(r, c + 2), device_id_type=MESH,
        )

    def cross_copy(s, side):
        return pltpu.make_async_remote_copy(
            dbuf.at[side, s], dbuf.at[side, s], d_send.at[1, s], d_recv.at[1, s],
            device_id=(r, cross), device_id_type=MESH,
        )

    def line_need(col, s):
        return (col >= 2) & (col < n_col) & (r + n_row * s >= col - col % 2)

    def cross_need(col, s):
        return (col >= 1) & (r + n_row * s >= col)

    def far_copy(k, q, source):
        target = r + 1 - 2 * (r % 2) if k == 0 else (r + 2 * k) % n_row
        return pltpu.make_async_remote_copy(
            source, far.at[q], far_send.at[k, q], far_recv.at[q],
            device_id=(target, c), device_id_type=MESH,
        )

    def arrive(s):
        @pl.when(cross_need(c, s))
        def _():
            cross_copy(s, 1 - x).wait_recv()

        @pl.when((c >= 1) & (r == far_row) & (far_slot == s))
        def _():
            for q in range(2):
                for k in range(n_row // 2):
                    far_copy(k, q, dbuf.at[q, s]).start()
                far[q] = dbuf[q, s]

    for s in range(slots):

        @pl.when(line_need(c, s))
        def _():
            line_copy(s).wait_recv()

        @pl.when(line_need(c + 2, s))
        def _():
            line_copy(s).start()

        @pl.when(cross_need(cross, s))
        def _():
            cross_copy(s, x).start()

        arrive(s)

    child = [
        ((r % 2 == 0) & (c == 0) & (r + 2 < n_row), (r + 2, c)),
        ((r % 2 == 0) & (c + 2 < n_col), (r, c + 2)),
        ((r % 2 == 0) & (c == 0), (r, c + 1)),
        ((r % 2 == 0) & (r + 1 < n_row), (r + 1, c)),
    ]

    def bc_copy(q, h, k):
        piece = bc.at[q, pl.ds(h * half, half)]
        return pltpu.make_async_remote_copy(
            piece, piece, bc_send.at[q, h, k], bc_recv.at[q, h],
            device_id=child[k][1], device_id_type=MESH,
        )

    def bc_start(q, h):
        for k in range(4):

            @pl.when(child[k][0])
            def _():
                bc_copy(q, h, k).start()

    def pass_on(q):
        for h in range(2):

            @pl.when(jnp.logical_not(root))
            def _():
                bc_copy(q, h, 0).wait_recv()
                bc_start(q, h)

    @pl.when(root)
    def _():
        first = inverse_factor(m_ref[0])
        bc[0] = first
        bc_start(0, 0)
        bc_start(0, 1)
        lead_copy(0).wait_recv()
        lead_copy(1).wait_recv()
        p01 = nt(lead[0], first)
        bc[1] = p01
        bc_start(1, 0)
        bc_start(1, 1)
        bc[2] = inverse_factor(lead[1] - nt(p01, p01))
        bc_start(2, 0)
        bc_start(2, 1)

    @pl.when((c >= 1) & (r != far_row))
    def _():
        for q in range(2):
            far_copy(0, q, far.at[q]).wait_recv()

            @pl.when(r % 2 == far_row % 2)
            def _():
                far_copy(0, q, far.at[q]).start()

    pass_on(0)
    pass_on(1)

    lower = lax.broadcasted_iota(jnp.int32, (width, width), 0) >= lax.broadcasted_iota(
        jnp.int32, (width, width), 1
    )

    @pl.when(c >= 2)
    def _():
        p0far[...] = nt(far[0], bc[0])
        wfar[...] = far[1] - nt(p0far[...], bc[1])

    for s in range(slots):
        inside = r + n_row * s >= c

        @pl.when(inside & (c == 0))
        def _():
            panel = nt(m_ref[s], bc[0])
            panel = jnp.where(lower | (r + n_row * s > 0), panel, 0.0)
            o_ref[s] = jnp.where(listed[s] > 0, panel, 0.0)

        @pl.when(inside & (c >= 1))
        def _():
            panel = nt(dbuf[0, s], bc[0])
            wcol[s] = dbuf[1, s] - nt(panel, bc[1])

            @pl.when(c >= 2)
            def _():
                product = nt(panel, p0far[...])
                acc[s] = m_ref[s] - jnp.where(update[s] > 0, product, 0.0)

    pass_on(2)

    @pl.when(c >= 2)
    def _():
        p1far = nt(wfar[...], bc[2])
        p0far[...] = nn(p1far, bc[2])

    for s in range(slots):
        inside = r + n_row * s >= c

        @pl.when(inside & (c == 1))
        def _():
            panel = nt(wcol[s], bc[2])
            panel = jnp.where(lower | (r + n_row * s > 1), panel, 0.0)
            o_ref[s] = jnp.where(listed[s] > 0, panel, 0.0)

        @pl.when(inside & (c >= 2))
        def _():
            product = nt(wcol[s], p0far[...])
            out = acc[s] - jnp.where(update[slots + s] > 0, product, 0.0)
            o_ref[s] = jnp.where(listed[s] > 0, out, 0.0)

        @pl.when(jnp.logical_not(inside))
        def _():
            o_ref[s] = jnp.zeros((width, width), jnp.float32)

    @pl.when(lead_a)
    def _():
        lead_copy(0).wait_send()

    @pl.when(lead_b)
    def _():
        lead_copy(1).wait_send()

    for s in range(slots):

        @pl.when(line_need(c + 2, s))
        def _():
            line_copy(s).wait_send()

        @pl.when(cross_need(cross, s))
        def _():
            cross_copy(s, x).wait_send()

    @pl.when((c >= 1) & (r == far_row))
    def _():
        for k in range(n_row // 2):
            for q in range(2):
                far_copy(k, q, dbuf.at[q, far_slot]).wait_send()

    @pl.when((c >= 1) & (r != far_row) & (r % 2 == far_row % 2))
    def _():
        for q in range(2):
            far_copy(0, q, far.at[q]).wait_send()

    for q in range(3):
        for h in range(2):
            for k in range(4):

                @pl.when(child[k][0])
                def _():
                    bc_copy(q, h, k).wait_send()


def on_device(n_row, n_col, matrix, present, update):
    tiles = matrix[:, 0, 0]
    slots, width = tiles.shape[0], tiles.shape[-1]
    tile = (width, width)
    dma = pltpu.SemaphoreType.DMA
    vmem = pl.BlockSpec(memory_space=pltpu.VMEM)
    smem = pl.BlockSpec(memory_space=pltpu.SMEM)
    out = pl.pallas_call(
        functools.partial(kernel, n_row, n_col),
        out_shape=jax.ShapeDtypeStruct(tiles.shape, jnp.float32),
        in_specs=[vmem, smem, smem],
        out_specs=vmem,
        scratch_shapes=[
            pltpu.VMEM((2, slots) + tile, jnp.float32),
            pltpu.VMEM((2,) + tile, jnp.float32),
            pltpu.VMEM((2,) + tile, jnp.float32),
            pltpu.VMEM((3,) + tile, jnp.float32),
            pltpu.VMEM((slots,) + tile, jnp.float32),
            pltpu.VMEM((slots,) + tile, jnp.float32),
            pltpu.VMEM(tile, jnp.float32),
            pltpu.VMEM(tile, jnp.float32),
            dma((2, slots)),
            dma((2, slots)),
            dma((n_row, 2)),
            dma((2,)),
            dma((2,)),
            dma((2,)),
            dma((3, 2, 4)),
            dma((3, 2)),
        ],
        compiler_params=pltpu.CompilerParams(
            collective_id=0, has_side_effects=True, vmem_limit_bytes=40 * 1024 * 1024
        ),
    )(tiles, present.reshape(slots), update.reshape(2 * slots))
    return out[:, None, None]


def solution(mesh):
    return jax.shard_map(
        functools.partial(on_device, mesh.shape["row"], mesh.shape["col"]),
        mesh=mesh,
        in_specs=(
            P(None, "row", "col", None, None),
            P(None, "row", "col"),
            P(None, None, "row", "col"),
        ),
        out_specs=P(None, "row", "col", None, None),
        check_vma=False,
    )
```
